32 devices in a mesh: cell: 16 (over z, y, core), tm: 2 (over x).
Axes of the slice: x: 2, y: 2, z: 4, core: 2. Of those that a mesh axis runs over, the one named last changes fastest.
Arguments:
- sketch: bfloat16 [16384, 256], P('cell', 'tm'), may hold values from -6 to 6
- tiles: bfloat16 [4, 384, 128, 128], P('tm', 'cell'), may hold values from -0.21875 to 0.21875
- row_counts: int32 [4, 16, 8], P('tm', 'cell'), may hold values from 1 to 6, 24 in all within a row
- col_index: int32 [4, 384], P('tm', 'cell'), may hold values from 0 to 127, as said below
- precision: float32 [4, 16384], P('tm', 'cell'), may hold values from 0.25 to 4
- prior: float32 [16384], P('cell'), may hold values from 0.5 to 2
Outputs:
- hessian_sketch: float32 [16384, 256], P('cell', 'tm')
The draws below stay inside these ranges and needn't reach their ends.
Inputs may be any that keep to these rules, and one draw needn't show every extreme that they name: `col_index`: in window w, tile k (device group d = k // 24) names a parameter block from d * 8 - 4 to d * 8 + 11 within the network; in every window each group has a tile at each of the two ends of that range that lie within the network. `row_counts`: the 8 counts of one group and window add up to 24; tiles are stored row block after row block.
All inputs are finite; a program needn't handle non-finite values.
Results may differ from the reference program's by a relative error of at most 0.00087.
Values may be sent and summed in bfloat16 or wider, within the bound.
A program may use at most 64 MiB of HBM per device.

```python
import math
import jax
import jax.numpy as jnp
import numpy as np
from jax import lax

BLK = 128
R = 256
PB_DEV = 8
HB = 4
RB = 8
MAXT = 6
NTD = 24
TWIN = 4
PBTOT = 128
PTOT = 16384
TILES = 384
ROWS = 16384
N_CELL = 16


def draw_col_index(key, part):
    key = jax.random.fold_in(key, 7)
    positions = jnp.arange(TILES, dtype=jnp.int32)
    group = positions // NTD
    within = positions % NTD
    offsets = jax.random.randint(key, (TWIN, TILES), -HB, PB_DEV + HB).astype(jnp.int32)
    offsets = jnp.where(within[None, :] == 0, -HB, offsets)
    offsets = jnp.where(within[None, :] == 1, PB_DEV + HB - 1, offsets)
    named = group[None, :] * PB_DEV + offsets
    return jnp.clip(named, 0, PBTOT - 1).astype(jnp.int32)


def block_levels(rng, dims, shards, low, largest):
    def one(axis_at, parts):
        draws = jax.random.uniform(jax.random.fold_in(jax.random.fold_in(rng, 6), axis_at), (parts,), jnp.float32, low / len(shards), largest / len(shards))
        return jnp.repeat(jnp.exp(draws), dims[axis_at] // parts).reshape((-1,) + (1,) * (len(dims) - axis_at - 1))

    loudness = one(*shards[0])
    for cut in shards[1:]:
        loudness = loudness * one(*cut)
    return loudness


def length_profile(amount, total, most, skew):
    weights = [(1 << 20) // math.isqrt(grade ** skew) + 1 for grade in range(2, amount + 1)]
    rest, counts = total - most - (amount - 1), [1] * (amount - 1)
    while rest > 0:
        movable = [i for i in range(amount - 1) if counts[i] < most]
        mass, remaining = sum([weights[i] for i in movable]), rest
        for i in movable:
            addition = min(most - counts[i], max(1, remaining * weights[i] // mass), rest)
            counts[i] = counts[i] + addition
            rest = rest - addition
    return np.array([most] + counts)


def uneven(rng, count, total, limit, slope):
    if count == 2:
        one = jax.random.randint(rng, (), max(1, total - limit), min(limit, total - 1) + 1)
        return jnp.stack([one, total - one])
    tallies = jnp.asarray(length_profile(count, total, limit, slope), jnp.int32)
    pairs = (count - 1) // 2
    source_of, sink = tallies[1:1 + 2 * pairs:2], tallies[2:2 + 2 * pairs:2]
    room = jnp.minimum(source_of - 1, limit - sink)
    passed = jax.random.randint(jax.random.fold_in(rng, 1), (pairs,), 0, 1 << 20) % (room + 1)
    tallies = tallies.at[1:1 + 2 * pairs:2].set(source_of - passed).at[2:2 + 2 * pairs:2].set(sink + passed)
    return tallies[jax.random.permutation(jax.random.fold_in(rng, 2), count)]


def normal_values(stream_key, dims, scale, reach, pieces=(), kind=jnp.bfloat16):
    values = scale * jax.random.normal(stream_key, dims, jnp.float32)
    if pieces:
        values = values * block_levels(stream_key, dims, pieces, -0.22, 0.18)
    return jnp.clip(values, -reach, reach).astype(kind)


def setup_inputs(seed: int = 0) -> dict:
    splits = jax.random.split(jax.random.key(seed), 7)
    return {
        "sketch": normal_values(splits[0], (PTOT, R), 1.0, 6.0, ((0, 16), (1, 2))),
        "tiles": normal_values(splits[1], (TWIN, TILES, BLK, BLK), (BLK * 6) ** -0.5, 0.21875, ((0, 2), (1, 16))),
        "row_counts": jax.vmap(lambda own: uneven(own, RB, NTD, MAXT, 2))(jax.random.split(splits[2], TWIN * N_CELL)).reshape((TWIN, N_CELL, RB)).astype(jnp.int32),
        "col_index": draw_col_index(jax.random.fold_in(splits[6], 71), 0),
        "precision": jnp.clip(jnp.exp(math.log(4.0) - 2.7725887 * jax.random.uniform(splits[4], (TWIN, ROWS), jnp.float32) ** block_levels(splits[4], (TWIN, ROWS), ((0, 2), (1, 16)), -0.2, 0.2)), 0.25, 4.0),
        "prior": jnp.clip(jnp.exp(math.log(2.0) - 1.3862944 * jax.random.uniform(splits[5], (PTOT,), jnp.float32) ** block_levels(splits[5], (PTOT,), ((0, 16),), -0.2, 0.2)), 0.5, 2.0),
    }


def reference(sketch, tiles, row_counts, col_index, precision, prior):
    blocks = sketch.reshape(PBTOT, BLK, R)
    tile_pos = jnp.arange(NTD, dtype=jnp.int32)
    group_first = RB * jnp.arange(N_CELL, dtype=jnp.int32)

    def window(total, items):
        tiles_here, counts_here, cols_here, weights_here = items
        row_ends = jnp.cumsum(counts_here, axis=-1).astype(jnp.int32)
        local_row = jnp.sum((tile_pos[None, :, None] >= row_ends[:, None, :]).astype(jnp.int32), axis=-1)
        tile_row = (local_row + group_first[:, None]).reshape(TILES).astype(jnp.int32)
        picked = blocks[cols_here].astype(jnp.float32)
        tiles_wide = tiles_here.astype(jnp.float32)
        products = jnp.einsum('tij,tjk->tik', tiles_wide, picked)
        forward = jax.ops.segment_sum(products, tile_row, num_segments=N_CELL * RB)
        weighted = (weights_here.reshape(N_CELL * RB, BLK, 1) * forward).astype(jnp.bfloat16)
        back = jnp.einsum('tij,tik->tjk', tiles_wide, weighted[tile_row].astype(jnp.float32))
        total = total + jax.ops.segment_sum(back, cols_here, num_segments=PBTOT)
        return total, None

    start = jnp.zeros((PBTOT, BLK, R), jnp.float32)
    curvature, unused = lax.scan(window, start, (tiles, row_counts, col_index, precision))
    return prior[:, None] * sketch.astype(jnp.float32) + curvature.reshape(PTOT, R)
```

```python
import functools

import jax
import jax.numpy as jnp
from jax import lax
from jax.experimental import pallas as pl
from jax.experimental.pallas import tpu as pltpu
from jax.sharding import PartitionSpec as P

HB = 4
MAXT = 6
MESH = pl.DeviceIdType.MESH


def kernel(
    n_cell, n_tm,
    counts_ref, cols_ref, sketch_ref, tiles_ref, precision_ref, out_ref,
    blocks, tiles_in, tiles_tr, levels, weighted, terms, edge_out, edge_in, own, parts,
    starts, tile_rows, earlier, latest,
    load_sem, x_send, x_recv, h_send, h_recv, e_send, e_recv, r_send, r_recv,
):
    windows, per_device = cols_ref.shape
    row_blocks = counts_ref.shape[-1]
    owned, size, width = sketch_ref.shape
    spread = owned + 2 * HB
    total = windows * per_device
    d, t = lax.axis_index("cell"), lax.axis_index("tm")
    first_block = d * owned - HB
    lower, upper = d > 0, d < n_cell - 1
    exists = (lower, upper)
    sides = (jnp.maximum(d - 1, 0), jnp.minimum(d + 1, n_cell - 1))
    peers = [lax.rem(t + o, n_tm) for o in range(1, n_tm)]
    senders = [lax.rem(t + n_tm - o, n_tm) for o in range(n_tm)]

    loads = [
        pltpu.make_async_copy(
            tiles_ref.at[pl.ds(w * per_device, per_device)],
            tiles_in.at[pl.ds(w * per_device, per_device)],
            load_sem.at[w],
        )
        for w in range(windows)
    ]
    loads.append(
        pltpu.make_async_copy(sketch_ref, blocks.at[t, pl.ds(HB, owned)], load_sem.at[windows])
    )
    for copy in loads:
        copy.start()

    barrier = pltpu.get_barrier_semaphore()
    for peer in peers:
        pl.semaphore_signal(barrier, inc=1, device_id=(d, peer), device_id_type=MESH)
    for h in range(2):
        @pl.when(exists[h])
        def _():
            pl.semaphore_signal(barrier, inc=1, device_id=(sides[h], t), device_id_type=MESH)
    waits = n_tm - 1 + lower.astype(jnp.int32) + upper.astype(jnp.int32)
    pl.semaphore_wait(barrier, waits)

    def x_copy(o, h):
        piece = pl.ds(h * (owned // 2), owned // 2)
        landing = pl.ds(HB + h * (owned // 2), owned // 2)
        return pltpu.make_async_remote_copy(
            src_ref=sketch_ref.at[piece],
            dst_ref=blocks.at[t, landing],
            send_sem=x_send.at[o - 1, h],
            recv_sem=x_recv.at[o - 1, h],
            device_id=(d, peers[o - 1]),
            device_id_type=MESH,
        )

    def x_arrival(o, h):
        landing = blocks.at[senders[o], pl.ds(HB + h * (owned // 2), owned // 2)]
        return pltpu.make_async_remote_copy(
            src_ref=landing, dst_ref=landing,
            send_sem=x_send.at[o - 1, h], recv_sem=x_recv.at[o - 1, h],
            device_id=(d, peers[o - 1]), device_id_type=MESH,
        )

    def h_copy(o, h):
        slot = senders[o]
        landing = blocks.at[slot, pl.ds((1 - h) * (spread - HB), HB)]
        if o == 0:
            source = sketch_ref.at[pl.ds(h * (owned - HB), HB)]
        else:
            source = blocks.at[slot, pl.ds(HB + h * (owned - HB), HB)]
        return pltpu.make_async_remote_copy(
            src_ref=source, dst_ref=landing,
            send_sem=h_send.at[o, h], recv_sem=h_recv.at[o, 1 - h],
            device_id=(sides[h], t), device_id_type=MESH,
        )

    def h_arrival(o, h):
        landing = blocks.at[senders[o], pl.ds(h * (spread - HB), HB)]
        return pltpu.make_async_remote_copy(
            src_ref=landing, dst_ref=landing,
            send_sem=h_send.at[o, h], recv_sem=h_recv.at[o, h],
            device_id=(sides[h], t), device_id_type=MESH,
        )

    for o in range(1, n_tm):
        for h in range(2):
            x_copy(o, h).start()
    for h in range(2):
        @pl.when(exists[h])
        def _():
            h_copy(0, h).start()

        @pl.when(jnp.logical_not(exists[h]))
        def _():
            for s in range(n_tm):
                blocks[s, pl.ds(h * (spread - HB), HB)] = jnp.zeros((HB, size, width), blocks.dtype)

    for w in range(windows):
        start = jnp.int32(0)
        ends = []
        for b in range(row_blocks):
            starts[w * row_blocks + b] = start
            start = start + counts_ref[w, 0, b]
            ends.append(start)

        def row_of(k, carry, w=w, ends=ends):
            row = jnp.int32(w * row_blocks)
            for b in range(row_blocks - 1):
                row = row + (k >= ends[b]).astype(jnp.int32)
            tile_rows[w * per_device + k] = row
            return carry

        lax.fori_loop(0, per_device, row_of, 0)

    last = tuple(jnp.int32(total) for _ in range(spread))
    for w in range(windows):
        def link(k, last, w=w):
            col = cols_ref[w, k] - first_block
            before = jnp.int32(total)
            for p in range(spread):
                before = jnp.where(col == p, last[p], before)
            earlier[w * per_device + k] = before
            return tuple(
                jnp.where(col == p, w * per_device + k, last[p]) for p in range(spread)
            )

        last = lax.fori_loop(0, per_device, link, last)
    for p in range(spread):
        latest[p] = last[p]

    terms[total] = jnp.zeros(terms.shape[1:], terms.dtype)

    def turn(k, carry):
        tiles_tr[k] = tiles_in[k].T
        return carry

    for w in range(windows):
        for b in range(row_blocks):
            level = precision_ref[w:w + 1, b * size:(b + 1) * size]
            levels[w * row_blocks + b] = jnp.broadcast_to(level, (size, size)).T

    loads[0].wait()
    lax.fori_loop(0, per_device, turn, 0)
    loads[windows].wait()
    for o in range(1, n_tm):
        for h in range(2):
            x_arrival(o, h).wait_recv()

            @pl.when(exists[h])
            def _():
                h_copy(o, h).start()

    for w in range(1, windows):
        loads[w].wait()
        lax.fori_loop(w * per_device, (w + 1) * per_device, turn, 0)
    for h in range(2):
        @pl.when(exists[h])
        def _():
            for o in range(n_tm):
                h_arrival(o, h).wait_recv()

    def forward(i, carry):
        w, b = i // row_blocks, i % row_blocks
        start, count = starts[i], counts_ref[w, 0, b]
        lhs, rhs = [], []
        for j in range(MAXT):
            k = jnp.minimum(start + j, per_device - 1)
            col = jnp.clip(cols_ref[w, k] - first_block, 0, spread - 1)
            tile = tiles_in[w * per_device + k]
            lhs.append(jnp.where(j < count, tile, jnp.zeros_like(tile)))
            rhs.append(jnp.concatenate([blocks[s, col] for s in range(n_tm)], axis=-1))
        product = jnp.dot(
            jnp.concatenate(lhs, axis=1), jnp.concatenate(rhs, axis=0),
            preferred_element_type=jnp.float32,
        )
        level = jnp.concatenate([levels[i]] * (width * n_tm // size), axis=1)
        weighted[i] = (level * product).astype(weighted.dtype)
        return carry

    lax.fori_loop(0, windows * row_blocks, forward, 0)

    unroll = 4

    def backward(i, carry):
        for u in range(unroll):
            k = i * unroll + u
            product = jnp.dot(
                tiles_tr[k], weighted[tile_rows[k]], preferred_element_type=jnp.float32
            )
            terms[k] = product + terms[earlier[k]]
        return carry

    lax.fori_loop(0, total // unroll, backward, 0)

    def e_copy(h):
        return pltpu.make_async_remote_copy(
            src_ref=edge_out.at[h], dst_ref=edge_in.at[1 - h],
            send_sem=e_send.at[h], recv_sem=e_recv.at[1 - h],
            device_id=(sides[h], t), device_id_type=MESH,
        )

    for h in range(2):
        @pl.when(exists[h])
        def _():
            for p in range(HB):
                value = terms[latest[h * (spread - HB) + p]]
                for s in range(n_tm):
                    edge_out[h, s, p] = value[:, s * width:(s + 1) * width]
            e_copy(h).start()

        @pl.when(jnp.logical_not(exists[h]))
        def _():
            edge_in[h] = jnp.zeros(edge_in.shape[1:], edge_in.dtype)

    for h in range(2):
        for p in range(owned // 2):
            value = terms[latest[HB + h * (owned // 2) + p]]
            for s in range(n_tm):
                own[h, s, p] = value[:, s * width:(s + 1) * width]

    def r_copy(o, h):
        return pltpu.make_async_remote_copy(
            src_ref=own.at[h, peers[o - 1]], dst_ref=parts.at[h, o - 1],
            send_sem=r_send.at[h, o - 1], recv_sem=r_recv.at[h, o - 1],
            device_id=(d, peers[o - 1]), device_id_type=MESH,
        )

    near = 1 - lax.rem(d, 2)
    order = (near, 1 - near)
    half = owned // 2

    def has(h):
        return jnp.where(h == 0, lower, upper)

    for h in order:
        @pl.when(has(h))
        def _():
            side = jnp.where(h == 0, sides[0], sides[1])
            pltpu.make_async_remote_copy(
                src_ref=edge_in.at[h], dst_ref=edge_in.at[h],
                send_sem=e_send.at[h], recv_sem=e_recv.at[h],
                device_id=(side, t), device_id_type=MESH,
            ).wait_recv()
        for o in range(1, n_tm):
            peer = peers[o - 1]
            for p in range(half):
                own[h, peer, p] = own[h, peer, p] + edge_in[h, peer, p]
            r_copy(o, h).start()
        for p in range(half):
            own[h, t, p] = own[h, t, p] + edge_in[h, t, p]

    for h in order:
        for o in range(1, n_tm):
            r_copy(o, h).wait_recv()
        for p in range(half):
            value = own[h, t, p]
            for o in range(1, n_tm):
                value = value + parts[h, o - 1, p]
            out_ref[h * half + p] = value

    for h in range(2):
        for o in range(1, n_tm):
            x_copy(o, h).wait_send()
            r_copy(o, h).wait_send()

        @pl.when(exists[h])
        def _():
            for o in range(n_tm):
                h_copy(o, h).wait_send()
            e_copy(h).wait_send()


def local(n_cell, n_tm, sketch, tiles, row_counts, col_index, precision, prior):
    windows, per_device, size, _ = tiles.shape
    rows, width = sketch.shape
    owned = rows // size
    row_blocks = row_counts.shape[-1]
    spread = owned + 2 * HB
    half = owned // 2
    total = windows * per_device
    columns = width * n_tm
    f32, bf16 = jnp.float32, jnp.bfloat16
    vmem, dma = pltpu.VMEM, pltpu.SemaphoreType.DMA
    curvature = pl.pallas_call(
        functools.partial(kernel, n_cell, n_tm),
        out_shape=jax.ShapeDtypeStruct((owned, size, width), f32),
        in_specs=[
            pl.BlockSpec(memory_space=pltpu.SMEM),
            pl.BlockSpec(memory_space=pltpu.SMEM),
            pl.BlockSpec(memory_space=pl.ANY),
            pl.BlockSpec(memory_space=pl.ANY),
            pl.BlockSpec(memory_space=pltpu.VMEM),
        ],
        out_specs=pl.BlockSpec(memory_space=pltpu.VMEM),
        scratch_shapes=[
            vmem((n_tm, spread, size, width), bf16),
            vmem((total, size, size), bf16),
            vmem((total, size, size), bf16),
            vmem((windows * row_blocks, size, size), f32),
            vmem((windows * row_blocks, size, columns), bf16),
            vmem((total + 1, size, columns), f32),
            vmem((2, n_tm, HB, size, width), f32),
            vmem((2, n_tm, HB, size, width), f32),
            vmem((2, n_tm, half, size, width), f32),
            vmem((2, max(n_tm - 1, 1), half, size, width), f32),
            pltpu.SMEM((windows * row_blocks,), jnp.int32),
            pltpu.SMEM((total,), jnp.int32),
            pltpu.SMEM((total,), jnp.int32),
            pltpu.SMEM((spread,), jnp.int32),
            dma((windows + 1,)),
            dma((n_tm, 2)),
            dma((n_tm, 2)),
            dma((n_tm, 2)),
            dma((n_tm, 2)),
            dma((2,)),
            dma((2,)),
            dma((2, n_tm)),
            dma((2, n_tm)),
        ],
        compiler_params=pltpu.CompilerParams(
            collective_id=0, has_side_effects=True, vmem_limit_bytes=48 * 2**20
        ),
        cost_estimate=pl.CostEstimate(
            flops=6 * total * size * size * columns,
            bytes_accessed=total * size * size * 2 + rows * width * 6,
            transcendentals=0,
        ),
    )(
        row_counts, col_index, sketch.reshape(owned, size, width),
        tiles.reshape(total, size, size), precision,
    )
    return prior[:, None] * sketch.astype(f32) + curvature.reshape(rows, width)


def solution(mesh):
    in_specs = (
        P("cell", "tm"),
        P("tm", "cell", None, None),
        P("tm", "cell", None),
        P("tm", "cell"),
        P("tm", "cell"),
        P("cell"),
    )
    out_specs = P("cell", "tm")
    body = functools.partial(local, mesh.shape["cell"], mesh.shape["tm"])
    return jax.shard_map(body, mesh=mesh, in_specs=in_specs, out_specs=out_specs, check_vma=False)
```

```python
import functools

import jax
import jax.numpy as jnp
from jax import lax
from jax.experimental import pallas as pl
from jax.experimental.pallas import tpu as pltpu
from jax.sharding import PartitionSpec as P

HB = 4
MAXT = 6
MESH = pl.DeviceIdType.MESH


def kernel(
    n_cell, n_tm,
    counts_hbm, cols_hbm, sketch_ref, tiles_ref, precision_hbm, out_ref,
    counts_ref, cols_ref, precision_ref,
    blocks, tiles_in, tiles_tr, levels, weighted, terms, own,
    edge_out, edge_in, parts_out, parts_in,
    edge_scale_out, edge_scale_in, parts_scale_out, parts_scale_in,
    starts, tile_rows, earlier, latest,
    load_sem, x_send, x_recv, h_send, h_recv, e_send, e_recv, r_send, r_recv,
):
    windows, per_device = cols_ref.shape
    row_blocks = counts_ref.shape[-1]
    owned, size, width = sketch_ref.shape
    spread = owned + 2 * HB
    total = windows * per_device
    d, t = lax.axis_index("cell"), lax.axis_index("tm")
    first_block = d * owned - HB
    lower, upper = d > 0, d < n_cell - 1
    exists = (lower, upper)
    sides = (jnp.maximum(d - 1, 0), jnp.minimum(d + 1, n_cell - 1))

    def has(h):
        return jnp.logical_or(
            jnp.logical_and(h == 0, lower), jnp.logical_and(h == 1, upper)
        )

    def side(h):
        return jnp.where(h == 0, sides[0], sides[1])

    peers = [lax.rem(t + o, n_tm) for o in range(1, n_tm)]
    senders = [lax.rem(t + n_tm - o, n_tm) for o in range(n_tm)]

    loads = [
        pltpu.make_async_copy(
            tiles_ref.at[pl.ds(w * per_device, per_device)],
            tiles_in.at[pl.ds(w * per_device, per_device)],
            load_sem.at[w],
        )
        for w in range(windows)
    ]
    loads.append(
        pltpu.make_async_copy(sketch_ref, blocks.at[t, pl.ds(HB, owned)], load_sem.at[windows])
    )
    small = [
        pltpu.make_async_copy(source, target, load_sem.at[windows + 1 + i])
        for i, (source, target) in enumerate(
            ((counts_hbm, counts_ref), (cols_hbm, cols_ref), (precision_hbm, precision_ref))
        )
    ]
    for copy in small + loads:
        copy.start()

    barrier = pltpu.get_barrier_semaphore()
    for peer in peers:
        pl.semaphore_signal(barrier, inc=1, device_id=(d, peer), device_id_type=MESH)
    for h in range(2):
        @pl.when(exists[h])
        def _():
            pl.semaphore_signal(barrier, inc=1, device_id=(sides[h], t), device_id_type=MESH)
    waits = n_tm - 1 + lower.astype(jnp.int32) + upper.astype(jnp.int32)
    pl.semaphore_wait(barrier, waits)

    def x_copy(o, h):
        piece = pl.ds(h * (owned // 2), owned // 2)
        landing = pl.ds(HB + h * (owned // 2), owned // 2)
        return pltpu.make_async_remote_copy(
            src_ref=sketch_ref.at[piece],
            dst_ref=blocks.at[t, landing],
            send_sem=x_send.at[o - 1, h],
            recv_sem=x_recv.at[o - 1, h],
            device_id=(d, peers[o - 1]),
            device_id_type=MESH,
        )

    def x_arrival(o, h):
        landing = blocks.at[senders[o], pl.ds(HB + h * (owned // 2), owned // 2)]
        return pltpu.make_async_remote_copy(
            src_ref=landing, dst_ref=landing,
            send_sem=x_send.at[o - 1, h], recv_sem=x_recv.at[o - 1, h],
            device_id=(d, peers[o - 1]), device_id_type=MESH,
        )

    def h_copy(o, h):
        slot = senders[o]
        landing = blocks.at[slot, pl.ds((1 - h) * (spread - HB), HB)]
        if o == 0:
            source = sketch_ref.at[pl.ds(h * (owned - HB), HB)]
        else:
            source = blocks.at[slot, pl.ds(HB + h * (owned - HB), HB)]
        return pltpu.make_async_remote_copy(
            src_ref=source, dst_ref=landing,
            send_sem=h_send.at[o, h], recv_sem=h_recv.at[o, 1 - h],
            device_id=(side(h), t), device_id_type=MESH,
        )

    def h_arrival(o, h):
        landing = blocks.at[senders[o], pl.ds(h * (spread - HB), HB)]
        return pltpu.make_async_remote_copy(
            src_ref=landing, dst_ref=landing,
            send_sem=h_send.at[o, h], recv_sem=h_recv.at[o, h],
            device_id=(side(h), t), device_id_type=MESH,
        )

    far = lax.rem(d, 2)
    near = 1 - far

    for h in (far, near):
        for o in range(1, n_tm):
            x_copy(o, h).start()

        @pl.when(has(h))
        def _():
            h_copy(0, h).start()

    for h in range(2):
        @pl.when(jnp.logical_not(exists[h]))
        def _():
            for s in range(n_tm):
                blocks[s, pl.ds(h * (spread - HB), HB)] = jnp.zeros((HB, size, width), blocks.dtype)

    for copy in small:
        copy.wait()

    for w in range(windows):
        start = jnp.int32(0)
        ends = []
        for b in range(row_blocks):
            starts[w * row_blocks + b] = start
            start = start + counts_ref[w, 0, b]
            ends.append(start)

        def row_of(k, carry, w=w, ends=ends):
            row = jnp.int32(w * row_blocks)
            for b in range(row_blocks - 1):
                row = row + (k >= ends[b]).astype(jnp.int32)
            tile_rows[w * per_device + k] = row
            return carry

        lax.fori_loop(0, per_device, row_of, 0)

    last = tuple(jnp.int32(total) for _ in range(spread))
    for w in range(windows):
        def link(k, last, w=w):
            col = cols_ref[w, k] - first_block
            before = jnp.int32(total)
            for p in range(spread):
                before = jnp.where(col == p, last[p], before)
            earlier[w * per_device + k] = before
            return tuple(
                jnp.where(col == p, w * per_device + k, last[p]) for p in range(spread)
            )

        last = lax.fori_loop(0, per_device, link, last)
    for p in range(spread):
        latest[p] = last[p]

    terms[total] = jnp.zeros(terms.shape[1:], terms.dtype)

    def turn(k, carry):
        tiles_tr[k] = tiles_in[k].T
        return carry

    for w in range(windows):
        for b in range(row_blocks):
            level = precision_ref[w:w + 1, b * size:(b + 1) * size]
            levels[w * row_blocks + b] = jnp.broadcast_to(level, (size, size)).T

    loads[windows].wait()
    for w, h in enumerate((far, near)):
        for o in range(1, n_tm):
            x_arrival(o, h).wait_recv()

            @pl.when(has(h))
            def _():
                h_copy(o, h).start()

        if w < windows:
            loads[w].wait()
            lax.fori_loop(w * per_device, (w + 1) * per_device, turn, 0)
    for w in range(2, windows):
        loads[w].wait()
        lax.fori_loop(w * per_device, (w + 1) * per_device, turn, 0)
    for h in range(2):
        @pl.when(exists[h])
        def _():
            for o in range(n_tm):
                h_arrival(o, h).wait_recv()

    def forward(i, carry):
        w, b = i // row_blocks, i % row_blocks
        start, count = starts[i], counts_ref[w, 0, b]
        lhs, rhs = [], []
        for j in range(MAXT):
            k = jnp.minimum(start + j, per_device - 1)
            col = jnp.clip(cols_ref[w, k] - first_block, 0, spread - 1)
            tile = tiles_in[w * per_device + k]
            lhs.append(jnp.where(j < count, tile, jnp.zeros_like(tile)))
            rhs.append(jnp.concatenate([blocks[s, col] for s in range(n_tm)], axis=-1))
        product = jnp.dot(
            jnp.concatenate(lhs, axis=1), jnp.concatenate(rhs, axis=0),
            preferred_element_type=jnp.float32,
        )
        level = jnp.concatenate([levels[i]] * (width * n_tm // size), axis=1)
        weighted[i] = (level * product).astype(weighted.dtype)
        return carry

    lax.fori_loop(0, windows * row_blocks, forward, 0)

    unroll = 4

    def backward(i, carry):
        for u in range(unroll):
            k = i * unroll + u
            product = jnp.dot(
                tiles_tr[k], weighted[tile_rows[k]], preferred_element_type=jnp.float32
            )
            terms[k] = product + terms[earlier[k]]
        return carry

    lax.fori_loop(0, total // unroll, backward, 0)

    def coded(value):
        largest = jnp.maximum(jnp.max(jnp.abs(value), axis=0, keepdims=True), 1e-33)
        code = jnp.round(value * (32000.0 / largest))
        return code.astype(jnp.int32).astype(jnp.int16), largest * (1.0 / 32000.0)

    def decoded(code, scale):
        return code.astype(jnp.int32).astype(jnp.float32) * scale

    slots = [t] + peers
    half = owned // 2

    def e_copies(o, h):
        return [
            pltpu.make_async_remote_copy(
                src_ref=out.at[h, slots[o]], dst_ref=landing.at[1 - h, slots[o]],
                send_sem=e_send.at[h, o, i], recv_sem=e_recv.at[1 - h, o, i],
                device_id=(side(h), t), device_id_type=MESH,
            )
            for i, (out, landing) in enumerate(
                ((edge_out, edge_in), (edge_scale_out, edge_scale_in))
            )
        ]

    def e_arrivals(o, h):
        return [
            pltpu.make_async_remote_copy(
                src_ref=landing.at[h, slots[o]], dst_ref=landing.at[h, slots[o]],
                send_sem=e_send.at[h, o, i], recv_sem=e_recv.at[h, o, i],
                device_id=(side(h), t), device_id_type=MESH,
            )
            for i, landing in enumerate((edge_in, edge_scale_in))
        ]

    def r_copies(o, h):
        return [
            pltpu.make_async_remote_copy(
                src_ref=out.at[h, o - 1], dst_ref=landing.at[h, o - 1],
                send_sem=r_send.at[h, o - 1, i], recv_sem=r_recv.at[h, o - 1, i],
                device_id=(d, peers[o - 1]), device_id_type=MESH,
            )
            for i, (out, landing) in enumerate(
                ((parts_out, parts_in), (parts_scale_out, parts_scale_in))
            )
        ]

    sequence = list(range(1, n_tm)) + [0]
    for h in (far, near):
        @pl.when(has(h))
        def _():
            for p in range(HB):
                code, scale = coded(terms[latest[h * (spread - HB) + p]])
                for s in range(n_tm):
                    edge_out[h, s, p] = code[:, s * width:(s + 1) * width]
                    edge_scale_out[h, s, pl.ds(p, 1)] = scale[:, s * width:(s + 1) * width]
            for o in sequence:
                for copy in e_copies(o, h):
                    copy.start()

        @pl.when(jnp.logical_not(has(h)))
        def _():
            edge_in[h] = jnp.zeros(edge_in.shape[1:], edge_in.dtype)
            edge_scale_in[h] = jnp.zeros(edge_scale_in.shape[1:], edge_scale_in.dtype)

    for h in range(2):
        for p in range(half):
            value = terms[latest[HB + h * half + p]]
            for s in range(n_tm):
                own[h, s, p] = value[:, s * width:(s + 1) * width]

    for h in (near, far):
        for o in range(1, n_tm):
            @pl.when(has(h))
            def _():
                for copy in e_arrivals(o, h):
                    copy.wait_recv()

            slot = slots[o]
            for p in range(half):
                value = own[h, slot, p] + decoded(
                    edge_in[h, slot, p], edge_scale_in[h, slot, pl.ds(p, 1)]
                )
                code, scale = coded(value)
                parts_out[h, o - 1, p] = code
                parts_scale_out[h, o - 1, pl.ds(p, 1)] = scale
            for copy in r_copies(o, h):
                copy.start()

    for h in (near, far):
        @pl.when(has(h))
        def _():
            for copy in e_arrivals(0, h):
                copy.wait_recv()

        for o in range(1, n_tm):
            for copy in r_copies(o, h):
                copy.wait_recv()
        for p in range(half):
            value = own[h, t, p] + decoded(edge_in[h, t, p], edge_scale_in[h, t, pl.ds(p, 1)])
            for o in range(1, n_tm):
                value = value + decoded(
                    parts_in[h, o - 1, p], parts_scale_in[h, o - 1, pl.ds(p, 1)]
                )
            out_ref[h * half + p] = value

    for h in (near, far):
        for o in range(1, n_tm):
            x_copy(o, h).wait_send()
            for copy in r_copies(o, h):
                copy.wait_send()

        @pl.when(has(h))
        def _():
            for o in range(n_tm):
                h_copy(o, h).wait_send()
                for copy in e_copies(o, h):
                    copy.wait_send()


def local(n_cell, n_tm, sketch, tiles, row_counts, col_index, precision, prior):
    windows, per_device, size, _ = tiles.shape
    rows, width = sketch.shape
    owned = rows // size
    row_blocks = row_counts.shape[-1]
    spread = owned + 2 * HB
    half = owned // 2
    total = windows * per_device
    columns = width * n_tm
    others = max(n_tm - 1, 1)
    f32, bf16, i16 = jnp.float32, jnp.bfloat16, jnp.int16
    vmem, dma = pltpu.VMEM, pltpu.SemaphoreType.DMA
    curvature = pl.pallas_call(
        functools.partial(kernel, n_cell, n_tm),
        out_shape=jax.ShapeDtypeStruct((owned, size, width), f32),
        in_specs=[
            pl.BlockSpec(memory_space=pl.ANY),
            pl.BlockSpec(memory_space=pl.ANY),
            pl.BlockSpec(memory_space=pl.ANY),
            pl.BlockSpec(memory_space=pl.ANY),
            pl.BlockSpec(memory_space=pl.ANY),
        ],
        out_specs=pl.BlockSpec(memory_space=pltpu.VMEM),
        scratch_shapes=[
            pltpu.SMEM(row_counts.shape, jnp.int32),
            pltpu.SMEM(col_index.shape, jnp.int32),
            vmem(precision.shape, f32),
            vmem((n_tm, spread, size, width), bf16),
            vmem((total, size, size), bf16),
            vmem((total, size, size), bf16),
            vmem((windows * row_blocks, size, size), f32),
            vmem((windows * row_blocks, size, columns), bf16),
            vmem((total + 1, size, columns), f32),
            vmem((2, n_tm, half, size, width), f32),
            vmem((2, n_tm, HB, size, width), i16),
            vmem((2, n_tm, HB, size, width), i16),
            vmem((2, others, half, size, width), i16),
            vmem((2, others, half, size, width), i16),
            vmem((2, n_tm, HB, width), f32),
            vmem((2, n_tm, HB, width), f32),
            vmem((2, others, half, width), f32),
            vmem((2, others, half, width), f32),
            pltpu.SMEM((windows * row_blocks,), jnp.int32),
            pltpu.SMEM((total,), jnp.int32),
            pltpu.SMEM((total,), jnp.int32),
            pltpu.SMEM((spread,), jnp.int32),
            dma((windows + 4,)),
            dma((n_tm, 2)),
            dma((n_tm, 2)),
            dma((n_tm, 2)),
            dma((n_tm, 2)),
            dma((2, n_tm, 2)),
            dma((2, n_tm, 2)),
            dma((2, n_tm, 2)),
            dma((2, n_tm, 2)),
        ],
        compiler_params=pltpu.CompilerParams(
            collective_id=0, has_side_effects=True, vmem_limit_bytes=60 * 2**20
        ),
        cost_estimate=pl.CostEstimate(
            flops=6 * total * size * size * columns,
            bytes_accessed=total * size * size * 2 + rows * width * 6,
            transcendentals=0,
        ),
    )(
        row_counts, col_index, sketch.reshape(owned, size, width),
        tiles.reshape(total, size, size), precision,
    )
    return prior[:, None] * sketch.astype(f32) + curvature.reshape(rows, width)


def solution(mesh):
    in_specs = (
        P("cell", "tm"),
        P("tm", "cell", None, None),
        P("tm", "cell", None),
        P("tm", "cell"),
        P("tm", "cell"),
        P("cell"),
    )
    out_specs = P("cell", "tm")
    body = functools.partial(local, mesh.shape["cell"], mesh.shape["tm"])
    return jax.shard_map(body, mesh=mesh, in_specs=in_specs, out_specs=out_specs, check_vma=False)
```

```python
import functools
import math

import jax
import jax.numpy as jnp
from jax import lax
from jax.experimental import pallas as pl
from jax.experimental.pallas import tpu as pltpu
from jax.sharding import PartitionSpec as P

HB = 4
MAXT = 6
MESH = pl.DeviceIdType.MESH


def kernel(
    n_cell, n_tm,
    counts_hbm, cols_hbm, sketch_ref, tiles_ref, precision_hbm, out_ref,
    counts_ref, cols_ref, precision_ref,
    my_blocks, blocks, tiles_in, tiles_tr, levels, my_weighted, their_weighted, my_terms, their_terms, own,
    edge_out, edge_in, parts_out, parts_in,
    edge_scale_out, edge_scale_in, parts_scale_out, parts_scale_in,
    starts, tile_rows, earlier, latest,
    load_sem, x_send, x_recv, h_send, h_recv, e_send, e_recv, r_send, r_recv,
):
    windows, per_device = cols_ref.shape
    row_blocks = counts_ref.shape[-1]
    owned, size, width = sketch_ref.shape
    spread = owned + 2 * HB
    total = windows * per_device
    d, t = lax.axis_index("cell"), lax.axis_index("tm")
    first_block = d * owned - HB
    lower, upper = d > 0, d < n_cell - 1
    exists = (lower, upper)
    sides = (jnp.maximum(d - 1, 0), jnp.minimum(d + 1, n_cell - 1))

    def has(h):
        return jnp.logical_or(
            jnp.logical_and(h == 0, lower), jnp.logical_and(h == 1, upper)
        )

    def side(h):
        return jnp.where(h == 0, sides[0], sides[1])

    peers = [lax.rem(t + o, n_tm) for o in range(1, n_tm)]
    senders = [lax.rem(t + n_tm - o, n_tm) for o in range(n_tm)]

    loads = [
        pltpu.make_async_copy(
            tiles_ref.at[pl.ds(w * per_device, per_device)],
            tiles_in.at[pl.ds(w * per_device, per_device)],
            load_sem.at[w],
        )
        for w in range(windows)
    ]
    loads.append(
        pltpu.make_async_copy(sketch_ref, my_blocks.at[pl.ds(HB, owned)], load_sem.at[windows])
    )
    small = [
        pltpu.make_async_copy(source, target, load_sem.at[windows + 1 + i])
        for i, (source, target) in enumerate(
            ((counts_hbm, counts_ref), (cols_hbm, cols_ref), (precision_hbm, precision_ref))
        )
    ]
    for copy in small + loads:
        copy.start()

    barrier = pltpu.get_barrier_semaphore()
    for peer in peers:
        pl.semaphore_signal(barrier, inc=1, device_id=(d, peer), device_id_type=MESH)
    for h in range(2):
        @pl.when(exists[h])
        def _():
            pl.semaphore_signal(barrier, inc=1, device_id=(sides[h], t), device_id_type=MESH)
    waits = n_tm - 1 + lower.astype(jnp.int32) + upper.astype(jnp.int32)
    pl.semaphore_wait(barrier, waits)

    def x_copy(o, h):
        piece = pl.ds(h * (owned // 2), owned // 2)
        landing = pl.ds(HB + h * (owned // 2), owned // 2)
        return pltpu.make_async_remote_copy(
            src_ref=sketch_ref.at[piece],
            dst_ref=blocks.at[t, landing],
            send_sem=x_send.at[o - 1, h],
            recv_sem=x_recv.at[o - 1, h],
            device_id=(d, peers[o - 1]),
            device_id_type=MESH,
        )

    def x_arrival(o, h):
        landing = blocks.at[senders[o], pl.ds(HB + h * (owned // 2), owned // 2)]
        return pltpu.make_async_remote_copy(
            src_ref=landing, dst_ref=landing,
            send_sem=x_send.at[o - 1, h], recv_sem=x_recv.at[o - 1, h],
            device_id=(d, peers[o - 1]), device_id_type=MESH,
        )

    def h_copy(o, h):
        slot = senders[o]
        margin = pl.ds((1 - h) * (spread - HB), HB)
        landing = blocks.at[slot, margin]
        if o == 0:
            landing = my_blocks.at[margin]
            source = sketch_ref.at[pl.ds(h * (owned - HB), HB)]
        else:
            source = blocks.at[slot, pl.ds(HB + h * (owned - HB), HB)]
        return pltpu.make_async_remote_copy(
            src_ref=source, dst_ref=landing,
            send_sem=h_send.at[o, h], recv_sem=h_recv.at[o, 1 - h],
            device_id=(side(h), t), device_id_type=MESH,
        )

    def h_arrival(o, h):
        margin = pl.ds(h * (spread - HB), HB)
        landing = blocks.at[senders[o], margin] if o else my_blocks.at[margin]
        return pltpu.make_async_remote_copy(
            src_ref=landing, dst_ref=landing,
            send_sem=h_send.at[o, h], recv_sem=h_recv.at[o, h],
            device_id=(side(h), t), device_id_type=MESH,
        )

    far = lax.rem(d, 2)
    near = 1 - far

    for h in (far, near):
        for o in range(1, n_tm):
            x_copy(o, h).start()

        @pl.when(has(h))
        def _():
            h_copy(0, h).start()

    for h in range(2):
        @pl.when(jnp.logical_not(exists[h]))
        def _():
            my_blocks[pl.ds(h * (spread - HB), HB)] = jnp.zeros((HB, size, width), blocks.dtype)
            for s in range(n_tm):
                blocks[s, pl.ds(h * (spread - HB), HB)] = jnp.zeros((HB, size, width), blocks.dtype)

    for copy in small:
        copy.wait()

    for w in range(windows):
        start = jnp.int32(0)
        ends = []
        for b in range(row_blocks):
            starts[w * row_blocks + b] = start
            start = start + counts_ref[w, 0, b]
            ends.append(start)

        def row_of(k, carry, w=w, ends=ends):
            row = jnp.int32(w * row_blocks)
            for b in range(row_blocks - 1):
                row = row + (k >= ends[b]).astype(jnp.int32)
            tile_rows[w * per_device + k] = row
            return carry

        lax.fori_loop(0, per_device, row_of, 0)

    last = tuple(jnp.int32(total) for _ in range(spread))
    for w in range(windows):
        def link(k, last, w=w):
            col = cols_ref[w, k] - first_block
            before = jnp.int32(total)
            for p in range(spread):
                before = jnp.where(col == p, last[p], before)
            earlier[w * per_device + k] = before
            return tuple(
                jnp.where(col == p, w * per_device + k, last[p]) for p in range(spread)
            )

        last = lax.fori_loop(0, per_device, link, last)
    for p in range(spread):
        latest[p] = last[p]

    for w in range(windows):
        for b in range(row_blocks):
            level = precision_ref[w:w + 1, b * size:(b + 1) * size]
            levels[w * row_blocks + b] = jnp.broadcast_to(level, (size, size)).T

    def turn(w):
        step = math.gcd(4, per_device)

        def some(i, carry):
            for u in range(step):
                k = w * per_device + i * step + u
                tiles_tr[k] = tiles_in[k].T
            return carry

        loads[w].wait()
        lax.fori_loop(0, per_device // step, some, 0)

    def forward(group, weighted):
        columns = weighted.shape[-1]
        step = math.gcd(2, windows * row_blocks)

        def some(n, carry):
            for u in range(step):
                i = n * step + u
                w, b = i // row_blocks, i % row_blocks
                start, count = starts[i], counts_ref[w, 0, b]
                lhs, rhs = [], []
                for j in range(MAXT):
                    k = jnp.minimum(start + j, per_device - 1)
                    col = jnp.clip(cols_ref[w, k] - first_block, 0, spread - 1)
                    tile = tiles_in[w * per_device + k]
                    lhs.append(jnp.where(j < count, tile, jnp.zeros_like(tile)))
                    parts = [blocks[slot, col] for slot in group] if group else [my_blocks[col]]
                    rhs.append(parts[0] if len(parts) == 1 else jnp.concatenate(parts, axis=-1))
                product = jnp.dot(
                    jnp.concatenate(lhs, axis=1), jnp.concatenate(rhs, axis=0),
                    preferred_element_type=jnp.float32,
                )
                level = jnp.concatenate([levels[i]] * -(-columns // size), axis=1)[:, :columns]
                weighted[i] = (level * product).astype(weighted.dtype)
            return carry

        lax.fori_loop(0, windows * row_blocks // step, some, 0)

    def backward(weighted, terms):
        step = math.gcd(8, total)

        def some(i, carry):
            for u in range(step):
                k = i * step + u
                product = jnp.dot(
                    tiles_tr[k], weighted[tile_rows[k]], preferred_element_type=jnp.float32
                )
                terms[k] = product + terms[earlier[k]]
            return carry

        lax.fori_loop(0, total // step, some, 0)

    def pass_on(h):
        for o in range(1, n_tm):
            x_arrival(o, h).wait_recv()

            @pl.when(has(h))
            def _():
                h_copy(o, h).start()

    def coded(value):
        largest = jnp.maximum(jnp.max(jnp.abs(value), axis=0, keepdims=True), 1e-33)
        code = jnp.round(value * (32000.0 / largest))
        return code.astype(jnp.int32).astype(jnp.int16), largest * (1.0 / 32000.0)

    def decoded(code, scale):
        return code.astype(jnp.int32).astype(jnp.float32) * scale

    slots = [t] + peers
    half = owned // 2

    def e_copies(o, h):
        return [
            pltpu.make_async_remote_copy(
                src_ref=out.at[h, slots[o]], dst_ref=landing.at[1 - h, slots[o]],
                send_sem=e_send.at[h, o, i], recv_sem=e_recv.at[1 - h, o, i],
                device_id=(side(h), t), device_id_type=MESH,
            )
            for i, (out, landing) in enumerate(
                ((edge_out, edge_in), (edge_scale_out, edge_scale_in))
            )
        ]

    def e_arrivals(o, h):
        return [
            pltpu.make_async_remote_copy(
                src_ref=landing.at[h, slots[o]], dst_ref=landing.at[h, slots[o]],
                send_sem=e_send.at[h, o, i], recv_sem=e_recv.at[h, o, i],
                device_id=(side(h), t), device_id_type=MESH,
            )
            for i, landing in enumerate((edge_in, edge_scale_in))
        ]

    def r_copies(o, h):
        return [
            pltpu.make_async_remote_copy(
                src_ref=out.at[h, o - 1], dst_ref=landing.at[h, o - 1],
                send_sem=r_send.at[h, o - 1, i], recv_sem=r_recv.at[h, o - 1, i],
                device_id=(d, peers[o - 1]), device_id_type=MESH,
            )
            for i, (out, landing) in enumerate(
                ((parts_out, parts_in), (parts_scale_out, parts_scale_in))
            )
        ]

    def send_edges(terms, group, h):
        @pl.when(has(h))
        def _():
            for p in range(HB):
                code, scale = coded(terms[latest[h * (spread - HB) + p]])
                for i, o in enumerate(group):
                    part = slice(i * width, (i + 1) * width)
                    edge_out[h, slots[o], p] = code[:, part]
                    edge_scale_out[h, slots[o], pl.ds(p, 1)] = scale[:, part]
            for o in group:
                for copy in e_copies(o, h):
                    copy.start()

    def keep(terms, group, h):
        for p in range(half):
            value = terms[latest[HB + h * half + p]]
            for i, o in enumerate(group):
                own[h, slots[o], p] = value[:, i * width:(i + 1) * width]

    mine, theirs = [0], list(range(1, n_tm))
    my_terms[total] = jnp.zeros(my_terms.shape[1:], my_terms.dtype)
    their_terms[total] = jnp.zeros(their_terms.shape[1:], their_terms.dtype)
    for h in range(2):
        @pl.when(jnp.logical_not(exists[h]))
        def _():
            edge_in[h] = jnp.zeros(edge_in.shape[1:], edge_in.dtype)
            edge_scale_in[h] = jnp.zeros(edge_scale_in.shape[1:], edge_scale_in.dtype)

    loads[windows].wait()
    turn(0)
    pass_on(far)
    for w in range(1, windows):
        turn(w)
    for h in range(2):
        @pl.when(exists[h])
        def _():
            h_arrival(0, h).wait_recv()
    forward([], my_weighted)
    pass_on(near)
    backward(my_weighted, my_terms)
    for h in (far, near):
        send_edges(my_terms, mine, h)

    for h in range(2):
        @pl.when(exists[h])
        def _():
            for o in theirs:
                h_arrival(o, h).wait_recv()
    if theirs:
        forward(peers, their_weighted)
        backward(their_weighted, their_terms)
        for h in (far, near):
            send_edges(their_terms, theirs, h)
        for h in (near, far):
            keep(their_terms, theirs, h)

    for h in (near, far):
        for o in range(1, n_tm):
            @pl.when(has(h))
            def _():
                for copy in e_arrivals(o, h):
                    copy.wait_recv()

            slot = slots[o]
            for p in range(half):
                value = own[h, slot, p] + decoded(
                    edge_in[h, slot, p], edge_scale_in[h, slot, pl.ds(p, 1)]
                )
                code, scale = coded(value)
                parts_out[h, o - 1, p] = code
                parts_scale_out[h, o - 1, pl.ds(p, 1)] = scale
            for copy in r_copies(o, h):
                copy.start()

    for h in (near, far):
        keep(my_terms, mine, h)
    for h in (near, far):
        @pl.when(has(h))
        def _():
            for copy in e_arrivals(0, h):
                copy.wait_recv()

        for o in range(1, n_tm):
            for copy in r_copies(o, h):
                copy.wait_recv()
        for p in range(half):
            value = own[h, t, p] + decoded(edge_in[h, t, p], edge_scale_in[h, t, pl.ds(p, 1)])
            for o in range(1, n_tm):
                value = value + decoded(
                    parts_in[h, o - 1, p], parts_scale_in[h, o - 1, pl.ds(p, 1)]
                )
            out_ref[h * half + p] = value

    for h in (near, far):
        for o in range(1, n_tm):
            x_copy(o, h).wait_send()
            for copy in r_copies(o, h):
                copy.wait_send()

        @pl.when(has(h))
        def _():
            for o in range(n_tm):
                h_copy(o, h).wait_send()
                for copy in e_copies(o, h):
                    copy.wait_send()


def local(n_cell, n_tm, sketch, tiles, row_counts, col_index, precision, prior):
    windows, per_device, size, _ = tiles.shape
    rows, width = sketch.shape
    owned = rows // size
    row_blocks = row_counts.shape[-1]
    spread = owned + 2 * HB
    half = owned // 2
    total = windows * per_device
    columns = width * n_tm
    others = max(n_tm - 1, 1)
    f32, bf16, i16 = jnp.float32, jnp.bfloat16, jnp.int16
    vmem, dma = pltpu.VMEM, pltpu.SemaphoreType.DMA
    curvature = pl.pallas_call(
        functools.partial(kernel, n_cell, n_tm),
        out_shape=jax.ShapeDtypeStruct((owned, size, width), f32),
        in_specs=[
            pl.BlockSpec(memory_space=pl.ANY),
            pl.BlockSpec(memory_space=pl.ANY),
            pl.BlockSpec(memory_space=pl.ANY),
            pl.BlockSpec(memory_space=pl.ANY),
            pl.BlockSpec(memory_space=pl.ANY),
        ],
        out_specs=pl.BlockSpec(memory_space=pltpu.VMEM),
        scratch_shapes=[
            pltpu.SMEM(row_counts.shape, jnp.int32),
            pltpu.SMEM(col_index.shape, jnp.int32),
            vmem(precision.shape, f32),
            vmem((spread, size, width), bf16),
            vmem((n_tm, spread, size, width), bf16),
            vmem((total, size, size), bf16),
            vmem((total, size, size), bf16),
            vmem((windows * row_blocks, size, size), f32),
            vmem((windows * row_blocks, size, width), bf16),
            vmem((windows * row_blocks, size, others * width), bf16),
            vmem((total + 1, size, width), f32),
            vmem((total + 1, size, others * width), f32),
            vmem((2, n_tm, half, size, width), f32),
            vmem((2, n_tm, HB, size, width), i16),
            vmem((2, n_tm, HB, size, width), i16),
            vmem((2, others, half, size, width), i16),
            vmem((2, others, half, size, width), i16),
            vmem((2, n_tm, HB, width), f32),
            vmem((2, n_tm, HB, width), f32),
            vmem((2, others, half, width), f32),
            vmem((2, others, half, width), f32),
            pltpu.SMEM((windows * row_blocks,), jnp.int32),
            pltpu.SMEM((total,), jnp.int32),
            pltpu.SMEM((total,), jnp.int32),
            pltpu.SMEM((spread,), jnp.int32),
            dma((windows + 4,)),
            dma((n_tm, 2)),
            dma((n_tm, 2)),
            dma((n_tm, 2)),
            dma((n_tm, 2)),
            dma((2, n_tm, 2)),
            dma((2, n_tm, 2)),
            dma((2, n_tm, 2)),
            dma((2, n_tm, 2)),
        ],
        compiler_params=pltpu.CompilerParams(
            collective_id=0, has_side_effects=True, vmem_limit_bytes=60 * 2**20
        ),
        cost_estimate=pl.CostEstimate(
            flops=6 * total * size * size * columns,
            bytes_accessed=total * size * size * 2 + rows * width * 6,
            transcendentals=0,
        ),
    )(
        row_counts, col_index, sketch.reshape(owned, size, width),
        tiles.reshape(total, size, size), precision,
    )
    return prior[:, None] * sketch.astype(f32) + curvature.reshape(rows, width)


def solution(mesh):
    in_specs = (
        P("cell", "tm"),
        P("tm", "cell", None, None),
        P("tm", "cell", None),
        P("tm", "cell"),
        P("tm", "cell"),
        P("cell"),
    )
    out_specs = P("cell", "tm")
    body = functools.partial(local, mesh.shape["cell"], mesh.shape["tm"])
    return jax.shard_map(body, mesh=mesh, in_specs=in_specs, out_specs=out_specs, check_vma=False)
```

```python
import functools
import math

import jax
import jax.numpy as jnp
from jax import lax
from jax.experimental import pallas as pl
from jax.experimental.pallas import tpu as pltpu
from jax.sharding import PartitionSpec as P

HB = 4
CUTS = 2
MAXT = 6
MESH = pl.DeviceIdType.MESH


def kernel(
    n_cell, n_tm,
    counts_hbm, cols_hbm, sketch_ref, tiles_ref, precision_hbm, out_ref,
    counts_ref, cols_ref, precision_ref,
    my_blocks, blocks, tiles_in, tiles_tr, levels, my_weighted, their_weighted, my_terms, their_terms, own,
    edge_out, edge_in, parts_out, parts_in,
    edge_scale_out, edge_scale_in, parts_scale_out, parts_scale_in,
    starts, tile_rows, earlier, latest,
    load_sem, x_send, x_recv, h_send, h_recv, e_send, e_recv, r_send, r_recv,
):
    windows, per_device = cols_ref.shape
    row_blocks = counts_ref.shape[-1]
    owned, size, width = sketch_ref.shape
    spread = owned + 2 * HB
    total = windows * per_device
    d, t = lax.axis_index("cell"), lax.axis_index("tm")
    first_block = d * owned - HB
    lower, upper = d > 0, d < n_cell - 1
    exists = (lower, upper)
    sides = (jnp.maximum(d - 1, 0), jnp.minimum(d + 1, n_cell - 1))

    def has(h):
        return jnp.logical_or(
            jnp.logical_and(h == 0, lower), jnp.logical_and(h == 1, upper)
        )

    def side(h):
        return jnp.where(h == 0, sides[0], sides[1])

    peers = [lax.rem(t + o, n_tm) for o in range(1, n_tm)]
    senders = [lax.rem(t + n_tm - o, n_tm) for o in range(n_tm)]

    loads = [
        pltpu.make_async_copy(
            tiles_ref.at[pl.ds(w * per_device, per_device)],
            tiles_in.at[pl.ds(w * per_device, per_device)],
            load_sem.at[w],
        )
        for w in range(windows)
    ]
    loads.append(
        pltpu.make_async_copy(sketch_ref, my_blocks.at[pl.ds(HB, owned)], load_sem.at[windows])
    )
    small = [
        pltpu.make_async_copy(source, target, load_sem.at[windows + 1 + i])
        for i, (source, target) in enumerate(
            ((counts_hbm, counts_ref), (cols_hbm, cols_ref), (precision_hbm, precision_ref))
        )
    ]
    for copy in small + loads:
        copy.start()

    barrier = pltpu.get_barrier_semaphore()
    for peer in peers:
        pl.semaphore_signal(barrier, inc=1, device_id=(d, peer), device_id_type=MESH)
    for h in range(2):
        @pl.when(exists[h])
        def _():
            pl.semaphore_signal(barrier, inc=1, device_id=(sides[h], t), device_id_type=MESH)
    waits = n_tm - 1 + lower.astype(jnp.int32) + upper.astype(jnp.int32)
    pl.semaphore_wait(barrier, waits)

    def x_copy(o, h):
        piece = pl.ds(h * (owned // 2), owned // 2)
        landing = pl.ds(HB + h * (owned // 2), owned // 2)
        return pltpu.make_async_remote_copy(
            src_ref=sketch_ref.at[piece],
            dst_ref=blocks.at[t, landing],
            send_sem=x_send.at[o - 1, h],
            recv_sem=x_recv.at[o - 1, h],
            device_id=(d, peers[o - 1]),
            device_id_type=MESH,
        )

    def x_arrival(o, h):
        landing = blocks.at[senders[o], pl.ds(HB + h * (owned // 2), owned // 2)]
        return pltpu.make_async_remote_copy(
            src_ref=landing, dst_ref=landing,
            send_sem=x_send.at[o - 1, h], recv_sem=x_recv.at[o - 1, h],
            device_id=(d, peers[o - 1]), device_id_type=MESH,
        )

    def h_copy(o, h):
        slot = senders[o]
        margin = pl.ds((1 - h) * (spread - HB), HB)
        landing = blocks.at[slot, margin]
        if o == 0:
            landing = my_blocks.at[margin]
            source = sketch_ref.at[pl.ds(h * (owned - HB), HB)]
        else:
            source = blocks.at[slot, pl.ds(HB + h * (owned - HB), HB)]
        return pltpu.make_async_remote_copy(
            src_ref=source, dst_ref=landing,
            send_sem=h_send.at[o, h], recv_sem=h_recv.at[o, 1 - h],
            device_id=(side(h), t), device_id_type=MESH,
        )

    def h_arrival(o, h):
        margin = pl.ds(h * (spread - HB), HB)
        landing = blocks.at[senders[o], margin] if o else my_blocks.at[margin]
        return pltpu.make_async_remote_copy(
            src_ref=landing, dst_ref=landing,
            send_sem=h_send.at[o, h], recv_sem=h_recv.at[o, h],
            device_id=(side(h), t), device_id_type=MESH,
        )

    far = lax.rem(d, 2)
    near = 1 - far

    for h in (far, near):
        for o in range(1, n_tm):
            x_copy(o, h).start()

        @pl.when(has(h))
        def _():
            h_copy(0, h).start()

    for h in range(2):
        @pl.when(jnp.logical_not(exists[h]))
        def _():
            my_blocks[pl.ds(h * (spread - HB), HB)] = jnp.zeros((HB, size, width), blocks.dtype)
            for s in range(n_tm):
                blocks[s, pl.ds(h * (spread - HB), HB)] = jnp.zeros((HB, size, width), blocks.dtype)

    for copy in small:
        copy.wait()

    for w in range(windows):
        start = jnp.int32(0)
        ends = []
        for b in range(row_blocks):
            starts[w * row_blocks + b] = start
            start = start + counts_ref[w, 0, b]
            ends.append(start)

        def row_of(k, carry, w=w, ends=ends):
            row = jnp.int32(w * row_blocks)
            for b in range(row_blocks - 1):
                row = row + (k >= ends[b]).astype(jnp.int32)
            tile_rows[w * per_device + k] = row
            return carry

        lax.fori_loop(0, per_device, row_of, 0)

    last = tuple(jnp.int32(total) for _ in range(spread))
    for w in range(windows):
        def link(k, last, w=w):
            col = cols_ref[w, k] - first_block
            before = jnp.int32(total)
            for p in range(spread):
                before = jnp.where(col == p, last[p], before)
            earlier[w * per_device + k] = before
            return tuple(
                jnp.where(col == p, w * per_device + k, last[p]) for p in range(spread)
            )

        last = lax.fori_loop(0, per_device, link, last)
    for p in range(spread):
        latest[p] = last[p]

    for w in range(windows):
        for b in range(row_blocks):
            level = precision_ref[w:w + 1, b * size:(b + 1) * size]
            levels[w * row_blocks + b] = jnp.broadcast_to(level, (size, size)).T

    def turn(w):
        step = math.gcd(4, per_device)

        def some(i, carry):
            for u in range(step):
                k = w * per_device + i * step + u
                tiles_tr[k] = tiles_in[k].T
            return carry

        loads[w].wait()
        lax.fori_loop(0, per_device // step, some, 0)

    def forward(group, weighted):
        columns = weighted.shape[-1]
        step = math.gcd(2, windows * row_blocks)

        def some(n, carry):
            for u in range(step):
                i = n * step + u
                w, b = i // row_blocks, i % row_blocks
                start, count = starts[i], counts_ref[w, 0, b]
                lhs, rhs = [], []
                for j in range(MAXT):
                    k = jnp.minimum(start + j, per_device - 1)
                    col = jnp.clip(cols_ref[w, k] - first_block, 0, spread - 1)
                    tile = tiles_in[w * per_device + k]
                    lhs.append(jnp.where(j < count, tile, jnp.zeros_like(tile)))
                    parts = [blocks[slot, col] for slot in group] if group else [my_blocks[col]]
                    rhs.append(parts[0] if len(parts) == 1 else jnp.concatenate(parts, axis=-1))
                product = jnp.dot(
                    jnp.concatenate(lhs, axis=1), jnp.concatenate(rhs, axis=0),
                    preferred_element_type=jnp.float32,
                )
                level = jnp.concatenate([levels[i]] * -(-columns // size), axis=1)[:, :columns]
                weighted[i] = (level * product).astype(weighted.dtype)
            return carry

        lax.fori_loop(0, windows * row_blocks // step, some, 0)

    def backward(weighted, terms):
        step = math.gcd(8, total)

        def some(i, carry):
            for u in range(step):
                k = i * step + u
                product = jnp.dot(
                    tiles_tr[k], weighted[tile_rows[k]], preferred_element_type=jnp.float32
                )
                terms[k] = product + terms[earlier[k]]
            return carry

        lax.fori_loop(0, total // step, some, 0)

    def pass_on(h):
        for o in range(1, n_tm):
            x_arrival(o, h).wait_recv()

            @pl.when(has(h))
            def _():
                h_copy(o, h).start()

    def coded(value):
        largest = jnp.maximum(jnp.max(jnp.abs(value), axis=0, keepdims=True), 1e-33)
        code = jnp.round(value * (32000.0 / largest))
        return code.astype(jnp.int32).astype(jnp.int16), largest * (1.0 / 32000.0)

    def decoded(code, scale):
        return code.astype(jnp.int32).astype(jnp.float32) * scale

    slots = [t] + peers
    half = owned // 2

    def cut(c):
        return pl.ds(c * (half // CUTS), half // CUTS)

    def e_copies(o, h, c):
        return [
            pltpu.make_async_remote_copy(
                src_ref=out.at[h, slots[o], cut(c)],
                dst_ref=landing.at[1 - h, slots[o], cut(c)],
                send_sem=e_send.at[h, o, i, c], recv_sem=e_recv.at[1 - h, o, i, c],
                device_id=(side(h), t), device_id_type=MESH,
            )
            for i, (out, landing) in enumerate(
                ((edge_out, edge_in), (edge_scale_out, edge_scale_in))
            )
        ]

    def e_arrivals(o, h, c):
        return [
            pltpu.make_async_remote_copy(
                src_ref=landing.at[h, slots[o], cut(c)],
                dst_ref=landing.at[h, slots[o], cut(c)],
                send_sem=e_send.at[h, o, i, c], recv_sem=e_recv.at[h, o, i, c],
                device_id=(side(h), t), device_id_type=MESH,
            )
            for i, landing in enumerate((edge_in, edge_scale_in))
        ]

    def r_copies(o, h, c):
        return [
            pltpu.make_async_remote_copy(
                src_ref=out.at[h, o - 1, cut(c)], dst_ref=landing.at[h, o - 1, cut(c)],
                send_sem=r_send.at[h, o - 1, i, c], recv_sem=r_recv.at[h, o - 1, i, c],
                device_id=(d, peers[o - 1]), device_id_type=MESH,
            )
            for i, (out, landing) in enumerate(
                ((parts_out, parts_in), (parts_scale_out, parts_scale_in))
            )
        ]

    def send_edges(terms, group, h):
        @pl.when(has(h))
        def _():
            for p in range(HB):
                code, scale = coded(terms[latest[h * (spread - HB) + p]])
                for i, o in enumerate(group):
                    part = slice(i * width, (i + 1) * width)
                    edge_out[h, slots[o], p] = code[:, part]
                    edge_scale_out[h, slots[o], p] = scale[:, part]
            for o in group:
                for c in range(CUTS):
                    for copy in e_copies(o, h, c):
                        copy.start()

    def keep(terms, group, h):
        for p in range(half):
            value = terms[latest[HB + h * half + p]]
            for i, o in enumerate(group):
                own[h, slots[o], p] = value[:, i * width:(i + 1) * width]

    mine, theirs = [0], list(range(1, n_tm))
    my_terms[total] = jnp.zeros(my_terms.shape[1:], my_terms.dtype)
    their_terms[total] = jnp.zeros(their_terms.shape[1:], their_terms.dtype)
    for h in range(2):
        @pl.when(jnp.logical_not(exists[h]))
        def _():
            edge_in[h] = jnp.zeros(edge_in.shape[1:], edge_in.dtype)
            edge_scale_in[h] = jnp.zeros(edge_scale_in.shape[1:], edge_scale_in.dtype)

    loads[windows].wait()
    turn(0)
    pass_on(far)
    for w in range(1, windows):
        turn(w)
    for h in range(2):
        @pl.when(exists[h])
        def _():
            h_arrival(0, h).wait_recv()
    forward([], my_weighted)
    pass_on(near)
    backward(my_weighted, my_terms)
    for h in (far, near):
        send_edges(my_terms, mine, h)

    for h in range(2):
        @pl.when(exists[h])
        def _():
            for o in theirs:
                h_arrival(o, h).wait_recv()
    if theirs:
        forward(peers, their_weighted)
        backward(their_weighted, their_terms)
        for h in (far, near):
            send_edges(their_terms, theirs, h)
        for h in (near, far):
            keep(their_terms, theirs, h)

    for h in (near, far):
        for o in theirs:
            slot = slots[o]
            for c in range(CUTS):
                @pl.when(has(h))
                def _():
                    for copy in e_arrivals(o, h, c):
                        copy.wait_recv()

                for p in range(c * (half // CUTS), (c + 1) * (half // CUTS)):
                    value = own[h, slot, p] + decoded(
                        edge_in[h, slot, p], edge_scale_in[h, slot, p]
                    )
                    code, scale = coded(value)
                    parts_out[h, o - 1, p] = code
                    parts_scale_out[h, o - 1, p] = scale
                for copy in r_copies(o, h, c):
                    copy.start()

    for h in (near, far):
        @pl.when(has(h))
        def _():
            for c in range(CUTS):
                for copy in e_arrivals(0, h, c):
                    copy.wait_recv()

        for p in range(half):
            own[h, t, p] = my_terms[latest[HB + h * half + p]] + decoded(
                edge_in[h, t, p], edge_scale_in[h, t, p]
            )

    for h in (near, far):
        for c in range(CUTS):
            for o in theirs:
                for copy in r_copies(o, h, c):
                    copy.wait_recv()
            for p in range(c * (half // CUTS), (c + 1) * (half // CUTS)):
                value = own[h, t, p]
                for o in theirs:
                    value = value + decoded(
                        parts_in[h, o - 1, p], parts_scale_in[h, o - 1, p]
                    )
                out_ref[h * half + p] = value

    for h in (near, far):
        for o in theirs:
            x_copy(o, h).wait_send()
            for c in range(CUTS):
                for copy in r_copies(o, h, c):
                    copy.wait_send()

        @pl.when(has(h))
        def _():
            for o in range(n_tm):
                h_copy(o, h).wait_send()
                for c in range(CUTS):
                    for copy in e_copies(o, h, c):
                        copy.wait_send()


def local(n_cell, n_tm, sketch, tiles, row_counts, col_index, precision, prior):
    windows, per_device, size, _ = tiles.shape
    rows, width = sketch.shape
    owned = rows // size
    row_blocks = row_counts.shape[-1]
    spread = owned + 2 * HB
    half = owned // 2
    total = windows * per_device
    columns = width * n_tm
    others = max(n_tm - 1, 1)
    f32, bf16, i16 = jnp.float32, jnp.bfloat16, jnp.int16
    vmem, dma = pltpu.VMEM, pltpu.SemaphoreType.DMA
    curvature = pl.pallas_call(
        functools.partial(kernel, n_cell, n_tm),
        out_shape=jax.ShapeDtypeStruct((owned, size, width), f32),
        in_specs=[
            pl.BlockSpec(memory_space=pl.ANY),
            pl.BlockSpec(memory_space=pl.ANY),
            pl.BlockSpec(memory_space=pl.ANY),
            pl.BlockSpec(memory_space=pl.ANY),
            pl.BlockSpec(memory_space=pl.ANY),
        ],
        out_specs=pl.BlockSpec(memory_space=pltpu.VMEM),
        scratch_shapes=[
            pltpu.SMEM(row_counts.shape, jnp.int32),
            pltpu.SMEM(col_index.shape, jnp.int32),
            vmem(precision.shape, f32),
            vmem((spread, size, width), bf16),
            vmem((n_tm, spread, size, width), bf16),
            vmem((total, size, size), bf16),
            vmem((total, size, size), bf16),
            vmem((windows * row_blocks, size, size), f32),
            vmem((windows * row_blocks, size, width), bf16),
            vmem((windows * row_blocks, size, others * width), bf16),
            vmem((total + 1, size, width), f32),
            vmem((total + 1, size, others * width), f32),
            vmem((2, n_tm, half, size, width), f32),
            vmem((2, n_tm, HB, size, width), i16),
            vmem((2, n_tm, HB, size, width), i16),
            vmem((2, others, half, size, width), i16),
            vmem((2, others, half, size, width), i16),
            vmem((2, n_tm, HB, 1, width), f32),
            vmem((2, n_tm, HB, 1, width), f32),
            vmem((2, others, half, 1, width), f32),
            vmem((2, others, half, 1, width), f32),
            pltpu.SMEM((windows * row_blocks,), jnp.int32),
            pltpu.SMEM((total,), jnp.int32),
            pltpu.SMEM((total,), jnp.int32),
            pltpu.SMEM((spread,), jnp.int32),
            dma((windows + 4,)),
            dma((n_tm, 2)),
            dma((n_tm, 2)),
            dma((n_tm, 2)),
            dma((n_tm, 2)),
            dma((2, n_tm, 2, CUTS)),
            dma((2, n_tm, 2, CUTS)),
            dma((2, n_tm, 2, CUTS)),
            dma((2, n_tm, 2, CUTS)),
        ],
        compiler_params=pltpu.CompilerParams(
            collective_id=0, has_side_effects=True, vmem_limit_bytes=60 * 2**20
        ),
        cost_estimate=pl.CostEstimate(
            flops=6 * total * size * size * columns,
            bytes_accessed=total * size * size * 2 + rows * width * 6,
            transcendentals=0,
        ),
    )(
        row_counts, col_index, sketch.reshape(owned, size, width),
        tiles.reshape(total, size, size), precision,
    )
    return prior[:, None] * sketch.astype(f32) + curvature.reshape(rows, width)


def solution(mesh):
    in_specs = (
        P("cell", "tm"),
        P("tm", "cell", None, None),
        P("tm", "cell", None),
        P("tm", "cell"),
        P("tm", "cell"),
        P("cell"),
    )
    out_specs = P("cell", "tm")
    body = functools.partial(local, mesh.shape["cell"], mesh.shape["tm"])
    return jax.shard_map(body, mesh=mesh, in_specs=in_specs, out_specs=out_specs, check_vma=False)
```
